32 devices in a mesh: row: 8 (over y, x, core), col: 4 (over z).
Axes of the slice: x: 2, y: 2, z: 4, core: 2. Of those that a mesh axis runs over, the one named last changes fastest.
Arguments:
- gate: bfloat16 [6144, 14336], P('row', 'col'), may hold values from -6 to 6
- up: bfloat16 [6144, 14336], P('row', 'col'), may hold values from -6 to 6
- out_grad: bfloat16 [6144, 4096], P('row', 'col'), may hold values from -6 to 6
- down_weight: bfloat16 [4096, 14336], P('row', 'col'), may hold values from -0.046875 to 0.046875
Outputs:
- gate_grad: bfloat16 [6144, 14336], P('row', 'col')
- up_grad: bfloat16 [6144, 14336], P('row', 'col')
- weight_grad: bfloat16 [4096, 14336], P('row', 'col')
The draws below stay inside these ranges and needn't reach their ends.
All inputs are finite; a program needn't handle non-finite values.
Results may differ from the reference program's by a relative error of at most 0.012.
Values may be sent and summed in bfloat16 or wider, within the bound.
A program may use at most 192 MiB of HBM per device.

```python
import jax
import jax.numpy as jnp
from jax import lax

D = 4096
FF = 14336
TOK_DEV = 768
TOKENS = 6144
N_ROW = 8


def strengthened(drawn, stream_key, source, target, blocks, factor):
    def block_of(position):
        return (jnp.arange(drawn.shape[position]) // (drawn.shape[position] // blocks)).reshape((-1,) + (1,) * (drawn.ndim - 1 - position))

    one_side = jax.random.permutation(stream_key, blocks)[block_of(target)]
    second = (block_of(target) + blocks // 2) % blocks
    return jnp.where((block_of(source) == one_side) | (block_of(source) == second), factor * drawn, drawn)


def levels(stream_key, shape, split, low, largest):
    factor_of, own = 1.0, jax.random.fold_in(stream_key, 6)
    for dim, shards_of in split:
        steps = jnp.exp(jax.random.uniform(jax.random.fold_in(own, dim), (shards_of,), jnp.float32, low / len(split), largest / len(split)))
        factor_of = factor_of * jnp.repeat(steps, shape[dim] // shards_of).reshape([-1 if axis == dim else 1 for axis in range(len(shape))])
    return factor_of


def scatter_about(stream_key, dims, deviation, most, split=(), held_as=jnp.bfloat16):
    array = deviation * jax.random.normal(stream_key, dims, jnp.float32)
    if split:
        array = array * levels(stream_key, dims, split, -0.22, 0.18)
    return jnp.clip(array, -most, most).astype(held_as)


def heavy_noise(stream_key, dims, deviation, most, shards, heavy, held_as=jnp.bfloat16):
    array = deviation * jax.random.normal(stream_key, dims, jnp.float32)
    if shards:
        array = array * levels(stream_key, dims, shards, -0.22, 0.18)
    return jnp.clip(strengthened(array, jax.random.fold_in(stream_key, 3), *heavy), -most, most).astype(held_as)


def setup_inputs(seed: int = 0) -> dict:
    seeds = jax.random.split(jax.random.key(seed), 5)
    gate = scatter_about(seeds[0], (TOKENS, FF), 1.5, 6.0, ((0, 8), (1, 4)))
    up = scatter_about(seeds[1], (TOKENS, FF), 1.0, 6.0, ((0, 8), (1, 4)))
    out_grad = heavy_noise(seeds[2], (TOKENS, D), 1.0, 6.0, ((0, 8), (1, 4)), (0, 1, 8, 2.0))
    down_weight = scatter_about(seeds[3], (D, FF), FF ** -0.5, 0.046875, ((0, 8), (1, 4)))
    return dict(gate=gate, up=up, out_grad=out_grad, down_weight=down_weight)


def reference(gate, up, out_grad, down_weight):
    gate_vals = gate.astype(jnp.float32)
    up_vals = up.astype(jnp.float32)
    sigma = jax.nn.sigmoid(gate_vals)
    activated = gate_vals * sigma
    hidden = (activated * up_vals).astype(jnp.bfloat16)
    hidden_grad = jnp.dot(out_grad, down_weight, preferred_element_type=jnp.float32)
    gate_grad = (hidden_grad * up_vals * sigma * (1.0 + gate_vals * (1.0 - sigma))).astype(jnp.bfloat16)
    up_grad = (hidden_grad * activated).astype(jnp.bfloat16)
    grad_scale = TOKENS ** -0.5

    def add_block(index_row, running):
        offset = (index_row * TOK_DEV).astype(jnp.int32)
        grad_block = lax.dynamic_slice_in_dim(out_grad, offset, TOK_DEV, 0)
        hidden_block = lax.dynamic_slice_in_dim(hidden, offset, TOK_DEV, 0)
        block_term = jnp.dot(grad_block.T, hidden_block, preferred_element_type=jnp.float32) * grad_scale
        rounded = lax.optimization_barrier(block_term.astype(jnp.bfloat16)).astype(jnp.float32)
        return running + rounded

    summed = lax.fori_loop(0, N_ROW, add_block, jnp.zeros((D, FF), jnp.float32))
    weight_grad = summed.astype(jnp.bfloat16)
    return (gate_grad, up_grad, weight_grad)
```

```python
import jax
import jax.numpy as jnp
from jax import lax
from jax.sharding import PartitionSpec as P

F32, BF16 = jnp.float32, jnp.bfloat16


def swap(value, mask):
    count = lax.axis_size("row")
    return lax.ppermute(value, "row", [(i, i ^ mask) for i in range(count)])


def gather_grad(out_grad):
    n = lax.axis_size("col")
    me = lax.axis_index("col")
    width = out_grad.shape[1]
    full = jnp.zeros((out_grad.shape[0], n * width), out_grad.dtype)
    block = out_grad
    full = lax.dynamic_update_slice(full, block, (0, me * width))
    for step in range(1, n):
        block = lax.ppermute(block, "col", [(i, (i + 1) % n) for i in range(n)])
        full = lax.dynamic_update_slice(full, block, (0, lax.rem(me - step + n, n) * width))
    return full


def gather_weight(w):
    half = w.shape[0] // 2
    wx = swap(w, 2)
    wy = swap(w, 4)
    da = swap(wx[:half], 4)
    db = swap(wy[half:], 2)
    own = {0: [w], 2: [wx], 4: [wy], 6: [da, db]}
    return {**own, **{m + 1: [swap(p, 1) for p in pieces] for m, pieces in own.items()}}


def per_device(gate, up, out_grad, down_weight):
    rows = lax.axis_size("row")
    tok_rows = gate.shape[0]
    grad_scale = (tok_rows * rows) ** (-0.5)
    gate_vals = gate.astype(F32)
    up_vals = up.astype(F32)
    sigma = jax.nn.sigmoid(gate_vals)
    activated = gate_vals * sigma
    hidden = lax.optimization_barrier((activated * up_vals).astype(BF16))
    if rows == 8:
        weight = gather_weight(down_weight)
        full_grad = gather_grad(out_grad)
        me = lax.axis_index("row")
        depth = down_weight.shape[0]
        half = depth // 2

        def columns(m):
            return lax.dynamic_slice_in_dim(full_grad, (me ^ m) * depth, depth, 1)

        def term(m):
            return (
                jnp.einsum("td,tf->df", columns(m), hidden, preferred_element_type=F32)
                * grad_scale
            ).astype(BF16)

        def add(a, b):
            return (a.astype(F32) + b.astype(F32)).astype(BF16)

        order = (6, 2, 4, 0)
        sent = {m: swap(term(m + 1), 1) for m in order}
        chip = {m: add(term(m), sent[m]) for m in order}
        ax = swap(chip[6][:half], 2)
        by = swap(chip[6][half:], 4)
        y_bot = swap(chip[4][half:], 4)
        x_top = swap(chip[2][:half], 2)
        y_top = swap(add(chip[4][:half], ax), 4)
        x_bot = swap(add(chip[2][half:], by), 2)
        own = chip[0].astype(F32)
        top = own[:half] + y_top.astype(F32) + x_top.astype(F32)
        bot = own[half:] + y_bot.astype(F32) + x_bot.astype(F32)
        summed = jnp.concatenate([top.astype(BF16), bot.astype(BF16)], axis=0)

        masks = (0, 1, 2, 3, 4, 5, 6, 7)
        grad_cols = jnp.concatenate([columns(m) for m in masks], axis=1)
        weights = jnp.concatenate([p for m in masks for p in weight[m]], axis=0)
        hidden_grad = jnp.dot(grad_cols, weights, preferred_element_type=F32)
    else:
        full_grad = lax.all_gather(out_grad, "col", axis=1, tiled=True)
        hidden_grad = jnp.dot(
            full_grad,
            lax.all_gather(down_weight, "row", axis=0, tiled=True),
            preferred_element_type=F32,
        )
        summed = lax.psum_scatter(
            (
                jnp.einsum("td,tf->df", full_grad, hidden, preferred_element_type=F32)
                * grad_scale
            ).astype(BF16),
            "row",
            scatter_dimension=0,
            tiled=True,
        )
    gate_grad = (hidden_grad * up_vals * sigma * (1.0 + gate_vals * (1.0 - sigma))).astype(BF16)
    up_grad = (hidden_grad * activated).astype(BF16)
    return (gate_grad, up_grad, summed)


def solution(mesh):
    in_specs = (P("row", "col"), P("row", "col"), P("row", "col"), P("row", "col"))
    out_specs = (P("row", "col"), P("row", "col"), P("row", "col"))
    return jax.shard_map(
        per_device, mesh=mesh, in_specs=in_specs, out_specs=out_specs, check_vma=False
    )
```

```python
import jax
import jax.numpy as jnp
from jax import lax
from jax.sharding import PartitionSpec as P

F32, BF16 = jnp.float32, jnp.bfloat16


def swap(value, mask):
    count = lax.axis_size("row")
    return lax.ppermute(value, "row", [(i, i ^ mask) for i in range(count)])


def gather_grad(out_grad):
    n = lax.axis_size("col")
    me = lax.axis_index("col")
    width = out_grad.shape[1]
    full = jnp.zeros((out_grad.shape[0], n * width), out_grad.dtype)
    block = out_grad
    full = lax.dynamic_update_slice(full, block, (0, me * width))
    hops = []
    for step in range(1, n):
        block = lax.ppermute(block, "col", [(i, (i + 1) % n) for i in range(n)])
        hops.append(block)
        full = lax.dynamic_update_slice(full, block, (0, lax.rem(me - step + n, n) * width))
    return full, hops


def gather_weight(w, hop):
    half = w.shape[0] // 2
    wx = swap(w, 2)
    wy = swap(w, 4)
    wx, wy, _ = lax.optimization_barrier((wx, wy, hop))
    da = swap(wx[:half], 4)
    db = swap(wy[half:], 2)
    own = {0: [w], 2: [wx], 4: [wy], 6: [da, db]}
    return {**own, **{m + 1: [swap(p, 1) for p in pieces] for m, pieces in own.items()}}


def per_device(gate, up, out_grad, down_weight):
    rows = lax.axis_size("row")
    tok_rows = gate.shape[0]
    grad_scale = (tok_rows * rows) ** (-0.5)
    gate_vals = gate.astype(F32)
    up_vals = up.astype(F32)
    sigma = jax.nn.sigmoid(gate_vals)
    activated = gate_vals * sigma
    hidden = lax.optimization_barrier((activated * up_vals).astype(BF16))
    if rows == 8:
        full_grad, hops = gather_grad(out_grad)
        weight = gather_weight(down_weight, hops[-2])
        me = lax.axis_index("row")
        depth = down_weight.shape[0]
        half = depth // 2

        def columns(m):
            return lax.dynamic_slice_in_dim(full_grad, (me ^ m) * depth, depth, 1)

        def term(m):
            return (
                jnp.einsum("td,tf->df", columns(m), hidden, preferred_element_type=F32)
                * grad_scale
            ).astype(BF16)

        def add(a, b):
            return (a.astype(F32) + b.astype(F32)).astype(BF16)

        order = (6, 2, 4, 0)
        sent = {m: swap(term(m + 1), 1) for m in order}
        chip = {m: add(term(m), sent[m]) for m in order}
        ax = swap(chip[6][:half], 2)
        by = swap(chip[6][half:], 4)
        y_bot = swap(chip[4][half:], 4)
        x_top = swap(chip[2][:half], 2)
        y_top = swap(add(chip[4][:half], ax), 4)
        x_bot = swap(add(chip[2][half:], by), 2)
        own = chip[0].astype(F32)
        top = own[:half] + y_top.astype(F32) + x_top.astype(F32)
        bot = own[half:] + y_bot.astype(F32) + x_bot.astype(F32)
        summed = jnp.concatenate([top.astype(BF16), bot.astype(BF16)], axis=0)

        weights = jnp.zeros((rows * depth, down_weight.shape[1]), BF16)
        for m in (0, 1, 2, 4, 3, 5, 6, 7):
            if m == 3:
                late = {k: weight[k] for k in (3, 5, 6, 7)}
                weights, late, full_grad, _ = lax.optimization_barrier(
                    (weights, late, full_grad, chip)
                )
                weight = {**weight, **late}
            offset = (me ^ m) * depth
            for piece in weight[m]:
                weights = lax.dynamic_update_slice(weights, piece, (offset, 0))
                offset = offset + piece.shape[0]
        hidden_grad = jnp.dot(full_grad, weights, preferred_element_type=F32)
    else:
        full_grad = lax.all_gather(out_grad, "col", axis=1, tiled=True)
        hidden_grad = jnp.dot(
            full_grad,
            lax.all_gather(down_weight, "row", axis=0, tiled=True),
            preferred_element_type=F32,
        )
        summed = lax.psum_scatter(
            (
                jnp.einsum("td,tf->df", full_grad, hidden, preferred_element_type=F32)
                * grad_scale
            ).astype(BF16),
            "row",
            scatter_dimension=0,
            tiled=True,
        )
    gate_grad = (hidden_grad * up_vals * sigma * (1.0 + gate_vals * (1.0 - sigma))).astype(BF16)
    up_grad = (hidden_grad * activated).astype(BF16)
    return (gate_grad, up_grad, summed)


def solution(mesh):
    in_specs = (P("row", "col"), P("row", "col"), P("row", "col"), P("row", "col"))
    out_specs = (P("row", "col"), P("row", "col"), P("row", "col"))
    return jax.shard_map(
        per_device, mesh=mesh, in_specs=in_specs, out_specs=out_specs, check_vma=False
    )
```

```python
import jax
import jax.numpy as jnp
from jax import lax
from jax.sharding import PartitionSpec as P

F32, BF16 = jnp.float32, jnp.bfloat16


def swap(value, mask):
    count = lax.axis_size("row")
    return lax.ppermute(value, "row", [(i, i ^ mask) for i in range(count)])


def gather_grad(out_grad):
    n = lax.axis_size("col")
    me = lax.axis_index("col")
    width = out_grad.shape[1]
    full = jnp.zeros((out_grad.shape[0], n * width), out_grad.dtype)
    block = out_grad
    full = lax.dynamic_update_slice(full, block, (0, me * width))
    hops = []
    for step in range(1, n):
        block = lax.ppermute(block, "col", [(i, (i + 1) % n) for i in range(n)])
        hops.append(block)
        full = lax.dynamic_update_slice(full, block, (0, lax.rem(me - step + n, n) * width))
    return full, hops


def gather_weight(w, hop):
    half = w.shape[0] // 2
    near = swap(w, 1)
    wx = swap(w, 2)
    wy = swap(w, 4)
    wx, wy, _ = lax.optimization_barrier((wx, wy, hop))
    da = swap(wx[:half], 4)
    db = swap(wy[half:], 2)
    return {0: [w], 1: [near], 2: [wx], 3: [swap(wx, 1)], 4: [wy], 5: [swap(wy, 1)], 6: [da, db]}


def per_device(gate, up, out_grad, down_weight):
    rows = lax.axis_size("row")
    tok_rows = gate.shape[0]
    grad_scale = (tok_rows * rows) ** (-0.5)
    gate_vals = gate.astype(F32)
    up_vals = up.astype(F32)
    sigma = jax.nn.sigmoid(gate_vals)
    activated = gate_vals * sigma
    hidden = lax.optimization_barrier((activated * up_vals).astype(BF16))
    if rows == 8:
        full_grad, hops = gather_grad(out_grad)
        weight = gather_weight(down_weight, hops[-2])
        me = lax.axis_index("row")
        depth = down_weight.shape[0]
        half = depth // 2

        def place(whole, shards):
            for m, pieces in shards.items():
                offset = (me ^ m) * depth
                for piece in pieces:
                    whole = lax.dynamic_update_slice(whole, piece, (offset, 0))
                    offset = offset + piece.shape[0]
            return whole

        weights = place(
            jnp.zeros((rows * depth, down_weight.shape[1]), BF16),
            {m: weight[m] for m in (0, 1, 2, 3, 4, 5)},
        )
        weights, weight[6], full_grad = lax.optimization_barrier((weights, weight[6], full_grad))
        weight[7] = [swap(piece, 1) for piece in weight[6]]

        def columns(m):
            return lax.dynamic_slice_in_dim(full_grad, (me ^ m) * depth, depth, 1)

        def term(m):
            return (
                jnp.einsum("td,tf->df", columns(m), hidden, preferred_element_type=F32)
                * grad_scale
            ).astype(BF16)

        def add(a, b):
            return (a.astype(F32) + b.astype(F32)).astype(BF16)

        sent = {m: swap(term(m + 1), 1) for m in (6, 4)}
        diagonal = add(term(6), sent[6])
        first = (diagonal[:half], diagonal[half:])
        first, weight[7], full_grad = lax.optimization_barrier((first, weight[7], full_grad))
        ax = swap(first[0], 2)
        by = swap(first[1], 4)
        sent.update({m: swap(term(m + 1), 1) for m in (2, 0)})
        chip = {m: add(term(m), sent[m]) for m in (4, 2, 0)}
        y_bot = swap(chip[4][half:], 4)
        x_top = swap(chip[2][:half], 2)
        y_top = swap(add(chip[4][:half], ax), 4)
        x_bot = swap(add(chip[2][half:], by), 2)
        own = chip[0].astype(F32)
        top = own[:half] + x_top.astype(F32)
        bot = own[half:] + y_bot.astype(F32)
        top, bot, y_top, x_bot = lax.optimization_barrier((top, bot, y_top, x_bot))
        summed = jnp.zeros((depth, down_weight.shape[1]), BF16)
        top = (top + y_top.astype(F32)).astype(BF16)
        bot = (bot + x_bot.astype(F32)).astype(BF16)
        summed = lax.dynamic_update_slice(summed, top, (0, 0))
        summed = lax.dynamic_update_slice(summed, bot, (half, 0))

        late = {k: weight[k] for k in (6, 7)}
        weights, late, full_grad, _ = lax.optimization_barrier((weights, late, full_grad, chip))
        weights = place(weights, late)
        hidden_grad = jnp.dot(full_grad, weights, preferred_element_type=F32)
    else:
        full_grad = lax.all_gather(out_grad, "col", axis=1, tiled=True)
        hidden_grad = jnp.dot(
            full_grad,
            lax.all_gather(down_weight, "row", axis=0, tiled=True),
            preferred_element_type=F32,
        )
        summed = lax.psum_scatter(
            (
                jnp.einsum("td,tf->df", full_grad, hidden, preferred_element_type=F32)
                * grad_scale
            ).astype(BF16),
            "row",
            scatter_dimension=0,
            tiled=True,
        )
    gate_grad = (hidden_grad * up_vals * sigma * (1.0 + gate_vals * (1.0 - sigma))).astype(BF16)
    up_grad = (hidden_grad * activated).astype(BF16)
    return (gate_grad, up_grad, summed)


def solution(mesh):
    in_specs = (P("row", "col"), P("row", "col"), P("row", "col"), P("row", "col"))
    out_specs = (P("row", "col"), P("row", "col"), P("row", "col"))
    return jax.shard_map(
        per_device, mesh=mesh, in_specs=in_specs, out_specs=out_specs, check_vma=False
    )
```

```python
import jax
import jax.numpy as jnp
from jax import lax
from jax.sharding import PartitionSpec as P

F32, BF16 = jnp.float32, jnp.bfloat16


def swap(value, mask):
    count = lax.axis_size("row")
    return lax.ppermute(value, "row", [(i, i ^ mask) for i in range(count)])


def gather_grad(out_grad):
    n = lax.axis_size("col")
    me = lax.axis_index("col")
    width = out_grad.shape[1]
    full = jnp.zeros((out_grad.shape[0], n * width), out_grad.dtype)
    block = out_grad
    full = lax.dynamic_update_slice(full, block, (0, me * width))
    hops = []
    for step in range(1, n):
        block = lax.ppermute(block, "col", [(i, (i + 1) % n) for i in range(n)])
        hops.append(block)
        full = lax.dynamic_update_slice(full, block, (0, lax.rem(me - step + n, n) * width))
    return full, hops


def gather_weight(w, hop):
    half = w.shape[0] // 2
    near = swap(w, 1)
    wx = swap(w, 2)
    wy = swap(w, 4)
    wx, wy, _ = lax.optimization_barrier((wx, wy, hop))
    da = swap(wx[:half], 4)
    db = swap(wy[half:], 2)
    return {0: [w], 1: [near], 2: [wx], 4: [wy], 6: [da, db]}


def per_device(gate, up, out_grad, down_weight):
    rows = lax.axis_size("row")
    tok_rows = gate.shape[0]
    grad_scale = (tok_rows * rows) ** (-0.5)
    gate_vals = gate.astype(F32)
    up_vals = up.astype(F32)
    sigma = jax.nn.sigmoid(gate_vals)
    activated = gate_vals * sigma
    hidden = lax.optimization_barrier((activated * up_vals).astype(BF16))
    if rows == 8:
        full_grad, hops = gather_grad(out_grad)
        weight = gather_weight(down_weight, hops[-2])
        me = lax.axis_index("row")
        depth = down_weight.shape[0]
        half = depth // 2

        def place(whole, shards):
            for m, pieces in shards.items():
                offset = (me ^ m) * depth
                for piece in pieces:
                    whole = lax.dynamic_update_slice(whole, piece, (offset, 0))
                    offset = offset + piece.shape[0]
            return whole

        weights = place(
            jnp.zeros((rows * depth, down_weight.shape[1]), BF16),
            {m: weight[m] for m in (0, 1, 2, 4)},
        )
        weights, weight, full_grad = lax.optimization_barrier((weights, weight, full_grad))

        def columns(m):
            return lax.dynamic_slice_in_dim(full_grad, (me ^ m) * depth, depth, 1)

        def term(m):
            return (
                jnp.einsum("td,tf->df", columns(m), hidden, preferred_element_type=F32)
                * grad_scale
            ).astype(BF16)

        def add(a, b):
            return (a.astype(F32) + b.astype(F32)).astype(BF16)

        sent = {m: swap(term(m + 1), 1) for m in (6, 4)}
        diagonal = add(term(6), sent[6])
        first = (diagonal[:half], diagonal[half:])
        first, full_grad, weights = lax.optimization_barrier((first, full_grad, weights))
        ax = swap(first[0], 2)
        by = swap(first[1], 4)
        sent.update({m: swap(term(m + 1), 1) for m in (2, 0)})
        chip = {m: add(term(m), sent[m]) for m in (4, 2, 0)}
        held, ax, by = lax.optimization_barrier(({m: weight[m] for m in (2, 4, 6)}, ax, by))
        weight.update({m + 1: [swap(p, 1) for p in held[m]] for m in (2, 4, 6)})
        y_bot = swap(chip[4][half:], 4)
        x_top = swap(chip[2][:half], 2)
        y_top = swap(add(chip[4][:half], ax), 4)
        x_bot = swap(add(chip[2][half:], by), 2)
        own = chip[0].astype(F32)
        top = own[:half] + x_top.astype(F32)
        bot = own[half:] + y_bot.astype(F32)
        late = {k: weight[k] for k in (3, 5, 6, 7)}
        weights, late, full_grad, _ = lax.optimization_barrier((weights, late, full_grad, chip))
        weights = place(weights, late)
        hidden_grad = jnp.dot(full_grad, weights, preferred_element_type=F32)
    else:
        full_grad = lax.all_gather(out_grad, "col", axis=1, tiled=True)
        hidden_grad = jnp.dot(
            full_grad,
            lax.all_gather(down_weight, "row", axis=0, tiled=True),
            preferred_element_type=F32,
        )
        summed = lax.psum_scatter(
            (
                jnp.einsum("td,tf->df", full_grad, hidden, preferred_element_type=F32)
                * grad_scale
            ).astype(BF16),
            "row",
            scatter_dimension=0,
            tiled=True,
        )
    gate_grad = (hidden_grad * up_vals * sigma * (1.0 + gate_vals * (1.0 - sigma))).astype(BF16)
    up_grad = (hidden_grad * activated).astype(BF16)
    if rows == 8:
        top, bot, y_top, x_bot, gate_grad, up_grad = lax.optimization_barrier(
            (top, bot, y_top, x_bot, gate_grad, up_grad)
        )
        summed = jnp.zeros((depth, down_weight.shape[1]), BF16)
        top = (top + y_top.astype(F32)).astype(BF16)
        bot = (bot + x_bot.astype(F32)).astype(BF16)
        summed = lax.dynamic_update_slice(summed, top, (0, 0))
        summed = lax.dynamic_update_slice(summed, bot, (half, 0))
    return (gate_grad, up_grad, summed)


def solution(mesh):
    in_specs = (P("row", "col"), P("row", "col"), P("row", "col"), P("row", "col"))
    out_specs = (P("row", "col"), P("row", "col"), P("row", "col"))
    return jax.shard_map(
        per_device, mesh=mesh, in_specs=in_specs, out_specs=out_specs, check_vma=False
    )
```
